512 devices in a mesh: pb: 32 (over z_hi, y, core), dev: 16 (over x, z_lo).
Axes of the slice: x: 4, y: 8, z: 8 (z_hi: 2, z_lo: 4; z = z_hi * 4 + z_lo), core: 2. Of those that a mesh axis runs over, the one named last changes fastest.
Arguments:
- query_factors: float32 [32768, 128], P('pb'), may hold values from -2.4 to 2.4
- panel_factors: float32 [131072, 128], P(('pb', 'dev')), may hold values from -2.4 to 2.4
- query_weight: float32 [32768], P('pb'), may hold values from 1 to 144, as said below
- plan: int32 [32], replicated, may hold values from 0 to 31, each once
- tile_seeds: int32 [32, 32], replicated, may hold values from 0 to 65520
Outputs:
- query_out: float32 [32768, 128], P('pb')
- panel_out: float32 [131072, 128], P(('pb', 'dev'))
The draws below stay inside these ranges and needn't reach their ends.
Inputs may be any that keep to these rules, and one draw needn't show every extreme that they name: `query_weight`: each row's weight is positive and at most 144.
All inputs are finite; a program needn't handle non-finite values.
Results may differ from the reference program's by a relative error of at most 0.00018.
Values sent between devices are 32-bit elements; how exact they have to be, the bound alone decides.
A program may use at most 64 MiB of HBM per device.

```python
import math
import jax
import jax.numpy as jnp
from jax import lax

QB = 1024
DC = 256
K = 128
STRATA = 3
PANELS = 32
QUERIES = 32768
DOCS = 131072
N_DEV = 16


def draw_query_weight(key, part):
    row_pos = jnp.arange(QUERIES, dtype=jnp.float32) / max(QUERIES - 1, 1)
    spread_log = jax.random.uniform(key, (QUERIES,), jnp.float32, 0.0, math.log(10.0))
    rising = 3.0 ** row_pos
    return (jnp.exp(spread_log) * rising).astype(jnp.float32)


def plant(entries, rng, low, high):
    shape = entries.shape
    place = [jax.random.randint(jax.random.fold_in(rng, axis), (), 0, shape[axis]) for axis in range(len(shape))]
    entries = entries.at[tuple(place)].set(low)
    longest = shape.index(max(shape))
    place[longest] = (place[longest] + 1) % shape[longest]
    return entries.at[tuple(place)].set(high)


def block_scale(rng, shape, cuts, least, largest):
    factor_of, own = 1.0, jax.random.fold_in(rng, 6)
    for axis_at, shards_of in cuts:
        heights = jnp.exp(jax.random.uniform(jax.random.fold_in(own, axis_at), (shards_of,), jnp.float32, least / len(cuts), largest / len(cuts)))
        factor_of = factor_of * jnp.repeat(heights, shape[axis_at] // shards_of).reshape([-1 if axis == axis_at else 1 for axis in range(len(shape))])
    return factor_of


def scatter_about(rng, shape, scale, reach, split=(), held_as=jnp.bfloat16):
    level = block_scale(rng, shape, split, -0.22, 0.18) if split else 1.0
    values = jax.random.normal(rng, shape, jnp.float32) * scale * level
    return jnp.minimum(jnp.maximum(values, -reach), reach).astype(held_as)


def setup_inputs(seed: int = 0) -> dict:
    arg_keys = jax.random.split(jax.random.key(seed), 6)
    return {
        "query_factors": scatter_about(arg_keys[0], (QUERIES, K), 0.3, 2.4, ((0, 32),), jnp.float32),
        "panel_factors": scatter_about(arg_keys[1], (DOCS, K), 0.3, 2.4, ((0, 512),), jnp.float32),
        "query_weight": draw_query_weight(jax.random.fold_in(arg_keys[5], 71), 0),
        "plan": jax.random.permutation(arg_keys[3], PANELS).astype(jnp.int32),
        "tile_seeds": plant(jax.random.randint(arg_keys[4], (PANELS, PANELS), 0, 65521), jax.random.fold_in(arg_keys[4], 1), 0, 65520).astype(jnp.int32),
    }


epsilon = 1e-06
learning_rate = 0.3

def shift_down(mixed, count):
    return lax.shift_right_logical(mixed, jnp.full(mixed.shape, count, jnp.int32))

def hashed(tile_seed, row_ids, col_ids):
    mixed = tile_seed * 374761393 + row_ids * 668265263 + col_ids * 1274126177
    mixed = mixed ^ shift_down(mixed, 15)
    mixed = mixed * 73244475
    mixed = mixed ^ shift_down(mixed, 13)
    mixed = mixed * 1911520717
    mixed = mixed ^ shift_down(mixed, 16)
    return (mixed & 65535).astype(jnp.float32) / 32768.0 - 1.0

def reference(query_factors, panel_factors, query_weight, plan, tile_seeds):
    groups = PANELS
    width = N_DEV * DC
    factors = query_factors.reshape(groups, QB, K)
    panels = panel_factors.reshape(groups, width, K)
    weights = query_weight.reshape(groups, QB)
    positions = jnp.arange(groups, dtype=jnp.int32)
    local_rows = jnp.arange(QB, dtype=jnp.int32)[:, None]
    local_cols = jnp.arange(width, dtype=jnp.int32)[None, :]
    for stratum in range(STRATA):
        panel_ids = plan[jnp.mod(positions - stratum, groups)]
        seed_list = tile_seeds[positions, panel_ids]

        def one_block(items):
            block_u, block_v, block_w, position, panel_id, tile_seed = items
            scores = hashed(tile_seed, position * QB + local_rows, panel_id * width + local_cols)
            approx = jnp.dot(block_u, block_v.T, precision=lax.Precision.HIGHEST)
            weighted = block_w[:, None] * (scores - approx)
            grad_u = jnp.dot(weighted, block_v, precision=lax.Precision.HIGHEST)
            grad_v = jnp.dot(weighted.T, block_u, precision=lax.Precision.HIGHEST)
            return (grad_u, grad_v)
        grad_u, grad_v = lax.map(one_block, (factors, panels, weights, positions, panel_ids, seed_list))
        factors = factors + learning_rate * grad_u / jnp.sqrt(jnp.mean(grad_u * grad_u) + epsilon)
        panels = panels + learning_rate * grad_v / jnp.sqrt(jnp.mean(grad_v * grad_v) + epsilon)
        panels = jnp.roll(panels, 1, axis=0)
    return (factors.reshape(QUERIES, K), panels.reshape(DOCS, K))
```

```python
import functools

import jax
import jax.numpy as jnp
from jax import lax
from jax.experimental import pallas as pl
from jax.experimental.pallas import tpu as pltpu
from jax.sharding import Mesh
from jax.sharding import PartitionSpec as P

STRATA = 3
PB = ("zh", "y", "c")
DEV = ("x", "z")
AXES = ("zh", "y", "c", "x", "z")
EPSILON = 1e-06
RATE = 0.3
MESH = pl.DeviceIdType.MESH
F32, BF16 = jnp.float32, jnp.bfloat16
ROWS, COLS, RANK = 1024, 256, 128
GROUPS = 32
WIDTH = 16 * COLS
GROUP_ROWS, SHARE = 256, 64


def ring_hops(d, n):
    return min(d, n - d)


YC = sorted(
    [(dy, dc) for dy in range(8) for dc in range(2) if dy or dc],
    key=lambda o: -(ring_hops(o[0], 8) + 0.5 * o[1]),
)
ZX = sorted(
    [(dz, dx) for dz in range(8) for dx in range(4) if dz or dx],
    key=lambda o: -(ring_hops(o[0], 8) + ring_hops(o[1], 4)),
)


def split(value):
    high = value.astype(BF16)
    return high, (value - high.astype(F32)).astype(BF16)


def dot3(a, b, dims):
    def dot(left, right):
        return lax.dot_general(left, right, (dims, ((), ())), preferred_element_type=F32)

    return dot(a[0], b[0]) + (dot(a[0], b[1]) + dot(a[1], b[0]))


def shift_down(mixed, count):
    return lax.shift_right_logical(mixed, jnp.full(mixed.shape, count, jnp.int32))


def hashed(mixed):
    mixed = mixed ^ shift_down(mixed, 15)
    mixed = mixed * 73244475
    mixed = mixed ^ shift_down(mixed, 13)
    mixed = mixed * 1911520717
    mixed = mixed ^ shift_down(mixed, 16)
    return (mixed & 65535).astype(F32) * (1.0 / 32768.0) - 1.0


def kernel(
    u_in, v_in, w_in, plan, seeds, u_out, v_out,
    scores, u_hi, u_lo, wu_hi, wu_lo, v_hi, v_lo, d_hi, d_lo, wide,
    r_buf, rx, z_src, rz, g_full, v_next, v_got, h_src, h_got,
    n_src, n1, n2_src, n2,
    rx_s, rx_r, rz_s, rz_r, az_s, az_r, ax_s, ax_r, sh_s, sh_r, n1_s, n1_r, n2_s, n2_r,
):
    zh, y, c, x, z = (lax.axis_index(a) for a in AXES)
    place = (zh * 8 + y) * 2 + c
    ring_z = zh * 4 + z

    def place_at(by):
        other = lax.rem(place + by + GROUPS, GROUPS)
        return (other // 16, lax.rem(other // 2, 8), lax.rem(other, 2), x, z)

    def yc(offset):
        return (zh, lax.rem(y + offset[0], 8), lax.rem(c + offset[1], 2), x, z)

    def zx(offset):
        other = lax.rem(ring_z + offset[0], 8)
        return (other // 4, y, c, lax.rem(x + offset[1], 4), lax.rem(other, 4))

    def x_at(k):
        return (zh, y, c, lax.rem(x + k, 4), z)

    def z_at(j):
        return (zh, y, c, x, z ^ j)

    def send(src, dst, s_sem, r_sem, device):
        copy = pltpu.make_async_remote_copy(
            src_ref=src, dst_ref=dst, send_sem=s_sem, recv_sem=r_sem,
            device_id=device, device_id_type=MESH,
        )
        copy.start()
        return copy

    barrier = pltpu.get_barrier_semaphore()
    for offset in YC:
        pl.semaphore_signal(barrier, inc=1, device_id=yc(offset), device_id_type=MESH)
    for offset in ZX:
        pl.semaphore_signal(barrier, inc=1, device_id=zx(offset), device_id_type=MESH)
    pl.semaphore_signal(barrier, inc=1, device_id=place_at(-1), device_id_type=MESH)

    for block in range(8):
        row = jnp.broadcast_to(w_in[block : block + 1, :], (128, 128))
        wide[block * 128 : (block + 1) * 128, :] = row.T

    def fill_scores(t):
        panel = plan[lax.rem(place - t + GROUPS, GROUPS)]
        seed = seeds[place, panel]
        first_col = panel * WIDTH + (x * 4 + z) * COLS
        base = seed * 374761393 + place * (ROWS * 668265263 % 2**32 - 2**32 * (ROWS * 668265263 % 2**32 >= 2**31))
        cols = (lax.broadcasted_iota(jnp.int32, (1, COLS), 1) + first_col) * 1274126177 + base
        for block in range(16):
            rows = (lax.broadcasted_iota(jnp.int32, (64, COLS), 0) + block * 64) * 668265263
            scores[t, block * 64 : (block + 1) * 64, :] = hashed(rows + cols)

    def keep_u(value):
        u_hi[...], u_lo[...] = split(value)
        wu_hi[...], wu_lo[...] = split(value * wide[...])

    keep_u(u_in[...])
    v_hi[...], v_lo[...] = split(v_in[...])
    fill_scores(0)
    own_rows = pl.multiple_of(z * GROUP_ROWS + x * SHARE, SHARE)
    after = place_at(1)
    barrier_due = True
    v_ref = v_in

    for t in range(STRATA):
        sent_x = []
        for j in (3, 2, 1, 0):
            first = pl.multiple_of((z ^ j) * GROUP_ROWS, GROUP_ROWS)
            rows = pl.ds(first, GROUP_ROWS)
            v = (v_hi[...], v_lo[...])
            approx = dot3((u_hi[rows, :], u_lo[rows, :]), v, ((1,), (1,)))
            d = split(scores[t, rows, :] - approx)
            d_hi[rows, :], d_lo[rows, :] = d
            r_buf[t, rows, :] = dot3(d, v, ((1,), (0,)))
            if barrier_due:
                pl.semaphore_wait(barrier, len(YC) + len(ZX) + 1)
                barrier_due = False
                sent_v = send(v_in, v_got.at[0], sh_s.at[0, 0], sh_r.at[0, 0], after)
            for k in (2, 1, 3):
                part = pl.ds(pl.multiple_of(first + lax.rem(x + k, 4) * SHARE, SHARE), SHARE)
                sent_x.append(
                    send(r_buf.at[t, part], rx.at[t, j, k - 1], rx_s.at[t, j, k - 1], rx_r.at[t, j, k - 1], x_at(k))
                )
        h = dot3((d_hi[...], d_lo[...]), (wu_hi[...], wu_lo[...]), ((0,), (0,)))
        h_src[t] = h
        sent_h = send(h_src.at[t], h_got.at[t], sh_s.at[t, 1], sh_r.at[t, 1], after)
        n_src[t, 1:2, :] = jnp.sum(h * h, axis=0, keepdims=True)
        if t + 1 < STRATA:
            fill_scores(t + 1)

        sent_z = []
        for j in (3, 2, 1, 0):
            for copy in sent_x[(3 - j) * 3 : (3 - j) * 3 + 3]:
                copy.wait_recv()
            part = pl.ds(pl.multiple_of((z ^ j) * GROUP_ROWS + x * SHARE, SHARE), SHARE)
            partial = r_buf[t, part, :] + (rx[t, j, 0] + rx[t, j, 1] + rx[t, j, 2])
            if j:
                z_src[t, j - 1] = partial
                sent_z.append(
                    send(z_src.at[t, j - 1], rz.at[t, j - 1], rz_s.at[t, j - 1], rz_r.at[t, j - 1], z_at(j))
                )
        for copy in sent_z:
            copy.wait_recv()
        own = pl.ds(own_rows, SHARE)
        g = wide[own, :] * (partial + (rz[t, 0] + rz[t, 1] + rz[t, 2]))
        g_full[t, own, :] = g
        n_src[t, 0:1, :] = jnp.sum(g * g, axis=0, keepdims=True)

        sent_1 = [send(n_src.at[t], n1.at[t, i], n1_s.at[t], n1_r.at[t], yc(o)) for i, o in enumerate(YC)]
        sent_az = [
            send(g_full.at[t, own], g_full.at[t, own], az_s.at[t, j - 1], az_r.at[t, j - 1], z_at(j)) for j in (3, 2, 1)
        ]
        sent_ax = [
            send(g_full.at[t, own], g_full.at[t, own], ax_s.at[t, 0, k - 1], ax_r.at[t, 0, k - 1], x_at(k))
            for k in (2, 1, 3)
        ]

        def forward(j):
            sent_az[3 - j].wait_recv()
            part = pl.ds(pl.multiple_of((z ^ j) * GROUP_ROWS + x * SHARE, SHARE), SHARE)
            for k in (2, 1, 3):
                sent_ax.append(
                    send(g_full.at[t, part], g_full.at[t, part], ax_s.at[t, j, k - 1], ax_r.at[t, j, k - 1], x_at(k))
                )

        forward(1)
        forward(2)
        every = pltpu.make_async_remote_copy(
            src_ref=n1.at[t], dst_ref=n1.at[t], send_sem=n1_s.at[t], recv_sem=n1_r.at[t],
            device_id=after, device_id_type=MESH,
        )
        every.wait_recv()
        total = n_src[t] + jnp.sum(n1[t], axis=0)
        n2_src[t] = total
        for i, o in enumerate(ZX):
            send(n2_src.at[t], n2.at[t, i], n2_s.at[t], n2_r.at[t], zx(o))
        forward(3)
        every.wait_send()
        for copy in sent_x + sent_z + sent_az + [sent_v, sent_h]:
            copy.wait_send()
        every = pltpu.make_async_remote_copy(
            src_ref=n2.at[t], dst_ref=n2.at[t], send_sem=n2_s.at[t], recv_sem=n2_r.at[t],
            device_id=after, device_id_type=MESH,
        )
        every.wait_recv()
        total = jnp.sum(total + jnp.sum(n2[t], axis=0), axis=1, keepdims=True)
        step_u = RATE / jnp.sqrt(total[0:1] / float(ROWS * GROUPS * RANK) + EPSILON)
        step_v = RATE / jnp.sqrt(total[1:2] / float(WIDTH * GROUPS * RANK) + EPSILON)
        sent_v.wait_recv()
        sent_h.wait_recv()
        v = v_got[t] + step_v * h_got[t]
        if t + 1 < STRATA:
            v_next[t] = v
            v_hi[...], v_lo[...] = split(v)
            sent_v = send(v_next.at[t], v_got.at[t + 1], sh_s.at[t + 1, 0], sh_r.at[t + 1, 0], after)
        else:
            v_out[...] = v
        for copy in sent_ax:
            copy.wait_recv()
        u = (u_in if t == 0 else u_out)[...] + step_u * g_full[t]
        u_out[...] = u
        if t + 1 < STRATA:
            keep_u(u)
        every.wait_send()
        for copy in sent_ax:
            copy.wait_send()


def per_device(query_factors, panel_factors, query_weight, plan, tile_seeds):
    vmem = pl.BlockSpec(memory_space=pltpu.VMEM)
    smem = pl.BlockSpec(memory_space=pltpu.SMEM)
    dma = pltpu.SemaphoreType.DMA
    T = STRATA
    return pl.pallas_call(
        kernel,
        out_shape=(
            jax.ShapeDtypeStruct((ROWS, RANK), F32),
            jax.ShapeDtypeStruct((COLS, RANK), F32),
        ),
        in_specs=[vmem, vmem, vmem, smem, smem],
        out_specs=(vmem, vmem),
        scratch_shapes=[
            pltpu.VMEM((T, ROWS, COLS), F32),
            pltpu.VMEM((ROWS, RANK), BF16),
            pltpu.VMEM((ROWS, RANK), BF16),
            pltpu.VMEM((ROWS, RANK), BF16),
            pltpu.VMEM((ROWS, RANK), BF16),
            pltpu.VMEM((COLS, RANK), BF16),
            pltpu.VMEM((COLS, RANK), BF16),
            pltpu.VMEM((ROWS, COLS), BF16),
            pltpu.VMEM((ROWS, COLS), BF16),
            pltpu.VMEM((ROWS, RANK), F32),
            pltpu.VMEM((T, ROWS, RANK), F32),
            pltpu.VMEM((T, 4, 3, SHARE, RANK), F32),
            pltpu.VMEM((T, 3, SHARE, RANK), F32),
            pltpu.VMEM((T, 3, SHARE, RANK), F32),
            pltpu.VMEM((T, ROWS, RANK), F32),
            pltpu.VMEM((T, COLS, RANK), F32),
            pltpu.VMEM((T, COLS, RANK), F32),
            pltpu.VMEM((T, COLS, RANK), F32),
            pltpu.VMEM((T, COLS, RANK), F32),
            pltpu.VMEM((T, 2, RANK), F32),
            pltpu.VMEM((T, len(YC), 2, RANK), F32),
            pltpu.VMEM((T, 2, RANK), F32),
            pltpu.VMEM((T, len(ZX), 2, RANK), F32),
            dma((T, 4, 3)), dma((T, 4, 3)),
            dma((T, 3)), dma((T, 3)),
            dma((T, 3)), dma((T, 3)),
            dma((T, 4, 3)), dma((T, 4, 3)),
            dma((T, 2)), dma((T, 2)),
            dma((T,)), dma((T,)),
            dma((T,)), dma((T,)),
        ],
        compiler_params=pltpu.CompilerParams(
            collective_id=0, has_side_effects=True, vmem_limit_bytes=40 * 2**20
        ),
        name="strata",
    )(query_factors, panel_factors, query_weight.reshape(8, 128), plan, tile_seeds)


def solution(mesh):
    finer = Mesh(mesh.devices.reshape(2, 8, 2, 4, 4), AXES)
    return jax.shard_map(
        per_device,
        mesh=finer,
        in_specs=(P(PB, None), P(PB + DEV, None), P(PB), P(), P()),
        out_specs=(P(PB, None), P(PB + DEV, None)),
        check_vma=False,
    )
```

```python
import functools

import jax
import jax.numpy as jnp
from jax import lax
from jax.experimental import pallas as pl
from jax.experimental.pallas import tpu as pltpu
from jax.sharding import Mesh
from jax.sharding import PartitionSpec as P

STRATA = 3
SUMS = 3
PB = ("zh", "y", "c")
DEV = ("x", "z")
AXES = ("zh", "y", "c", "x", "z")
EPSILON = 1e-06
RATE = 0.3
MESH = pl.DeviceIdType.MESH
F32, BF16 = jnp.float32, jnp.bfloat16
ROWS, COLS, RANK = 1024, 256, 128
GROUPS = 32
WIDTH = 16 * COLS
GROUP_ROWS, SHARE = 256, 64


def ring_hops(d, n):
    return min(d, n - d)


YC = sorted(
    [(dy, dc) for dy in range(8) for dc in range(2) if dy or dc],
    key=lambda o: -(ring_hops(o[0], 8) + 0.5 * o[1]),
)
ZX = sorted(
    [(dz, dx) for dz in range(8) for dx in range(4) if dz or dx],
    key=lambda o: -(ring_hops(o[0], 8) + ring_hops(o[1], 4)),
)


def split(value):
    high = value.astype(BF16)
    return high, (value - high.astype(F32)).astype(BF16)


def dot3(a, b, dims):
    def dot(left, right):
        return lax.dot_general(left, right, (dims, ((), ())), preferred_element_type=F32)

    return dot(a[0], b[0]) + (dot(a[0], b[1]) + dot(a[1], b[0]))


def shift_down(mixed, count):
    return lax.shift_right_logical(mixed, jnp.full(mixed.shape, count, jnp.int32))


def hashed(mixed):
    mixed = mixed ^ shift_down(mixed, 15)
    mixed = mixed * 73244475
    mixed = mixed ^ shift_down(mixed, 13)
    mixed = mixed * 1911520717
    mixed = mixed ^ shift_down(mixed, 16)
    return (mixed & 65535).astype(F32) * (1.0 / 32768.0) - 1.0


def kernel(
    u_hbm, v_hbm, w_hbm, plan_hbm, seeds_hbm, u_out, v_out,
    u_now, v_now, w_in, plan, seeds,
    scores, u_hi, u_lo, wu_hi, wu_lo, v_hi, v_lo, d_hi, d_lo, wide,
    r_buf, rx, z_src, rz, g_full, v_src, v_got, h_src, h_got,
    n1_src, n1, n2_src, n2,
    in_s, rx_s, rx_r, rz_s, rz_r, az_s, az_r, ax_s, ax_r, sh_s, sh_r, n1_s, n1_r, n2_s, n2_r,
):
    zh, y, c, x, z = (lax.axis_index(a) for a in AXES)
    place = (zh * 8 + y) * 2 + c
    ring_z = zh * 4 + z

    loads = [
        pltpu.make_async_copy(src, dst, in_s.at[i])
        for i, (src, dst) in enumerate(
            [(seeds_hbm, seeds), (plan_hbm, plan), (u_hbm, u_now), (v_hbm, v_now), (w_hbm, w_in)]
        )
    ]
    for load in loads:
        load.start()

    def place_at(by):
        other = lax.rem(place + by + GROUPS, GROUPS)
        return (other // 16, lax.rem(other // 2, 8), lax.rem(other, 2), x, z)

    def yc(offset):
        return (zh, lax.rem(y + offset[0], 8), lax.rem(c + offset[1], 2), x, z)

    def zx(offset):
        other = lax.rem(ring_z + offset[0], 8)
        return (other // 4, y, c, lax.rem(x + offset[1], 4), lax.rem(other, 4))

    def x_at(k):
        return (zh, y, c, lax.rem(x + k, 4), z)

    def z_at(j):
        return (zh, y, c, x, z ^ j)

    def remote(src, dst, s_sem, r_sem, device):
        return pltpu.make_async_remote_copy(
            src_ref=src, dst_ref=dst, send_sem=s_sem, recv_sem=r_sem,
            device_id=device, device_id_type=MESH,
        )

    pending = []

    def send(src, dst, s_sem, r_sem, device):
        copy = remote(src, dst, s_sem, r_sem, device)
        copy.start()
        pending.append(copy)
        return copy

    def settle():
        for copy in pending:
            copy.wait_send()
        pending.clear()

    barrier = pltpu.get_barrier_semaphore()
    for offset in ZX:
        pl.semaphore_signal(barrier, inc=1, device_id=zx(offset), device_id_type=MESH)
    for offset in YC:
        pl.semaphore_signal(barrier, inc=1, device_id=yc(offset), device_id_type=MESH)
    pl.semaphore_signal(barrier, inc=1, device_id=place_at(-1), device_id_type=MESH)
    for load in loads:
        load.wait()

    after = place_at(1)
    own = pl.ds(pl.multiple_of(z * GROUP_ROWS + x * SHARE, SHARE), SHARE)

    def group(j):
        first = pl.multiple_of((z ^ j) * GROUP_ROWS, GROUP_ROWS)
        return first, pl.ds(first, GROUP_ROWS)

    def part(j, k=0):
        return pl.ds(
            pl.multiple_of((z ^ j) * GROUP_ROWS + lax.rem(x + k, 4) * SHARE, SHARE), SHARE
        )

    def score_base(t):
        panel = plan[lax.rem(place - t + GROUPS, GROUPS)]
        seed = seeds[place, panel]
        first_col = panel * WIDTH + (x * 4 + z) * COLS
        base = seed * 374761393 + place * ROWS * 668265263
        return (lax.broadcasted_iota(jnp.int32, (1, COLS), 1) + first_col) * 1274126177 + base

    def score_rows(cols, first, count):
        rows = (lax.broadcasted_iota(jnp.int32, (count, COLS), 0) + first) * 668265263
        return hashed(rows + cols)

    def fill_scores(t):
        cols = score_base(t)
        for block in range(16):
            scores[t - 1, block * 64 : (block + 1) * 64, :] = score_rows(cols, block * 64, 64)

    def keep_u(value):
        u_hi[...], u_lo[...] = split(value)
        wu_hi[...], wu_lo[...] = split(value * wide[...])

    def keep_v(value):
        v_hi[...], v_lo[...] = split(value)

    def v_pair():
        return v_hi[...], v_lo[...]

    def residual(rows, score):
        d = split(score - dot3((u_hi[rows, :], u_lo[rows, :]), v_pair(), ((1,), (1,))))
        d_hi[rows, :], d_lo[rows, :] = d
        return d

    def grad_v():
        return dot3((d_hi[...], d_lo[...]), (wu_hi[...], wu_lo[...]), ((0,), (0,)))

    def send_x(t, j):
        return [
            send(r_buf.at[t, part(j, k)], rx.at[t, j, k - 1], rx_s.at[t, j, k - 1], rx_r.at[t, j, k - 1], x_at(k))
            for k in (2, 1, 3)
        ]

    def collect_x(t, sent_x):
        sent_z = []
        for j in (3, 2, 1, 0):
            for copy in sent_x[j]:
                copy.wait_recv()
            partial = r_buf[t, part(j), :] + (rx[t, j, 0] + rx[t, j, 1] + rx[t, j, 2])
            if j:
                z_src[t, j - 1] = partial
                sent_z.append(
                    send(z_src.at[t, j - 1], rz.at[t, j - 1], rz_s.at[t, j - 1], rz_r.at[t, j - 1], z_at(j))
                )
        return partial, sent_z

    def collect_z(t, partial, sent_z):
        for copy in sent_z:
            copy.wait_recv()
        return partial + (rz[t, 0] + rz[t, 1] + rz[t, 2])

    def gather_z(t):
        return {
            j: send(g_full.at[t, own], g_full.at[t, own], az_s.at[t, j - 1], az_r.at[t, j - 1], z_at(j))
            for j in (3, 2, 1)
        }

    def gather_x(t):
        return [
            send(g_full.at[t, own], g_full.at[t, own], ax_s.at[t, 0, k - 1], ax_r.at[t, 0, k - 1], x_at(k))
            for k in (2, 1, 3)
        ]

    def gather_start(t):
        return gather_z(t), gather_x(t)

    def gather_forward(t, state, j):
        to_z, to_x = state
        to_z[j].wait_recv()
        for k in (2, 1, 3):
            to_x.append(
                send(
                    g_full.at[t, part(j)], g_full.at[t, part(j)],
                    ax_s.at[t, j, k - 1], ax_r.at[t, j, k - 1], x_at(k),
                )
            )

    def gather_end(t, state):
        for copy in state[1]:
            copy.wait_recv()
        return g_full[t]

    def sum_first(i):
        for slot, o in enumerate(YC):
            remote(n1_src.at[i], n1.at[i, slot], n1_s.at[i], n1_r.at[i], yc(o)).start()

    def sum_wait(i, landed, s_sem, r_sem):
        every = remote(landed.at[i], landed.at[i], s_sem.at[i], r_sem.at[i], after)
        every.wait_recv()
        pending.append(every)
        return jnp.sum(landed[i], axis=0)

    def sum_second(i):
        n2_src[i] = n1_src[i] + sum_wait(i, n1, n1_s, n1_r)
        for slot, o in enumerate(ZX):
            remote(n2_src.at[i], n2.at[i, slot], n2_s.at[i], n2_r.at[i], zx(o)).start()

    def sum_end(i):
        return jnp.sum(n2_src[i] + sum_wait(i, n2, n2_s, n2_r), axis=1, keepdims=True)

    def step_u(total):
        return RATE / jnp.sqrt(total[0:1] / float(ROWS * GROUPS * RANK) + EPSILON)

    def step_v(total):
        return RATE / jnp.sqrt(total[1:2] / float(WIDTH * GROUPS * RANK) + EPSILON)

    def squares(value):
        return jnp.sum(value * value, axis=0, keepdims=True)

    for block in range(8):
        row = jnp.broadcast_to(w_in[block : block + 1, :], (128, 128))
        wide[block * 128 : (block + 1) * 128, :] = row.T
    keep_u(u_now[...])
    keep_v(v_now[...])

    for t in range(STRATA):
        if t == 0:
            cols = score_base(0)
        else:
            sent_v = send(v_src.at[t] if t else v_now, v_got.at[t], sh_s.at[t, 0], sh_r.at[t, 0], after)
        sent_x = {}
        for j in (3, 2, 1, 0):
            first, rows = group(j)
            score = scores[t - 1, rows, :] if t else score_rows(cols, first, GROUP_ROWS)
            d = residual(rows, score)
            r_buf[t, rows, :] = dot3(d, v_pair(), ((1,), (0,)))
            if t == 0 and j == 3:
                pl.semaphore_wait(barrier, len(YC) + len(ZX) + 1)
                sent_v = send(v_now, v_got.at[0], sh_s.at[0, 0], sh_r.at[0, 0], after)
            sent_x[j] = send_x(t, j)
        h = grad_v()
        h_src[t] = h
        n1_src[t, 1:2, :] = squares(h)
        sent_h = send(h_src.at[t], h_got.at[t], sh_s.at[t, 1], sh_r.at[t, 1], after)
        if t + 1 < STRATA:
            fill_scores(t + 1)
        partial, sent_z = collect_x(t, sent_x)
        g = wide[own, :] * collect_z(t, partial, sent_z)
        g_full[t, own, :] = g
        n1_src[t, 0:1, :] = squares(g)
        sum_first(t)
        gather = gather_start(t)
        gather_forward(t, gather, 1)
        gather_forward(t, gather, 2)
        sum_second(t)
        gather_forward(t, gather, 3)
        settle()
        sent_v.wait_recv()
        sent_h.wait_recv()
        g = gather_end(t, gather)
        total = sum_end(t)
        v = v_got[t] + step_v(total) * h_got[t]
        u = u_now[...] + step_u(total) * g
        if t + 1 < STRATA:
            v_src[t + 1] = v
            keep_v(v)
            u_now[...] = u
            keep_u(u)
        else:
            v_out[...] = v
            u_out[...] = u
    settle()


def per_device(query_factors, panel_factors, query_weight, plan, tile_seeds):
    vmem = pl.BlockSpec(memory_space=pltpu.VMEM)
    anywhere = pl.BlockSpec(memory_space=pl.ANY)
    dma = pltpu.SemaphoreType.DMA
    T = STRATA
    return pl.pallas_call(
        kernel,
        out_shape=(
            jax.ShapeDtypeStruct((ROWS, RANK), F32),
            jax.ShapeDtypeStruct((COLS, RANK), F32),
        ),
        in_specs=[anywhere] * 5,
        out_specs=(vmem, vmem),
        scratch_shapes=[
            pltpu.VMEM((ROWS, RANK), F32),
            pltpu.VMEM((COLS, RANK), F32),
            pltpu.VMEM((8, RANK), F32),
            pltpu.SMEM((GROUPS,), jnp.int32),
            pltpu.SMEM((GROUPS, GROUPS), jnp.int32),
            pltpu.VMEM((T - 1, ROWS, COLS), F32),
            pltpu.VMEM((ROWS, RANK), BF16),
            pltpu.VMEM((ROWS, RANK), BF16),
            pltpu.VMEM((ROWS, RANK), BF16),
            pltpu.VMEM((ROWS, RANK), BF16),
            pltpu.VMEM((COLS, RANK), BF16),
            pltpu.VMEM((COLS, RANK), BF16),
            pltpu.VMEM((ROWS, COLS), BF16),
            pltpu.VMEM((ROWS, COLS), BF16),
            pltpu.VMEM((ROWS, RANK), F32),
            pltpu.VMEM((T, ROWS, RANK), F32),
            pltpu.VMEM((T, 4, 3, SHARE, RANK), F32),
            pltpu.VMEM((T, 3, SHARE, RANK), F32),
            pltpu.VMEM((T, 3, SHARE, RANK), F32),
            pltpu.VMEM((T, ROWS, RANK), F32),
            pltpu.VMEM((T, COLS, RANK), F32),
            pltpu.VMEM((T, COLS, RANK), F32),
            pltpu.VMEM((T, COLS, RANK), F32),
            pltpu.VMEM((T, COLS, RANK), F32),
            pltpu.VMEM((SUMS, 2, RANK), F32),
            pltpu.VMEM((SUMS, len(YC), 2, RANK), F32),
            pltpu.VMEM((SUMS, 2, RANK), F32),
            pltpu.VMEM((SUMS, len(ZX), 2, RANK), F32),
            dma((5,)),
            dma((T, 4, 3)), dma((T, 4, 3)),
            dma((T, 3)), dma((T, 3)),
            dma((T, 3)), dma((T, 3)),
            dma((T, 4, 3)), dma((T, 4, 3)),
            dma((T, 2)), dma((T, 2)),
            dma((SUMS,)), dma((SUMS,)),
            dma((SUMS,)), dma((SUMS,)),
        ],
        compiler_params=pltpu.CompilerParams(
            collective_id=0, has_side_effects=True, vmem_limit_bytes=56 * 2**20
        ),
        name="strata",
    )(query_factors, panel_factors, query_weight.reshape(8, 128), plan, tile_seeds)


def solution(mesh):
    finer = Mesh(mesh.devices.reshape(2, 8, 2, 4, 4), AXES)
    return jax.shard_map(
        per_device,
        mesh=finer,
        in_specs=(P(PB, None), P(PB + DEV, None), P(PB), P(), P()),
        out_specs=(P(PB, None), P(PB + DEV, None)),
        check_vma=False,
    )
```

```python
import functools

import jax
import jax.numpy as jnp
from jax import lax
from jax.experimental import pallas as pl
from jax.experimental.pallas import tpu as pltpu
from jax.sharding import Mesh
from jax.sharding import PartitionSpec as P

STRATA = 3
SUMS = 3
PB = ("zh", "y", "c")
DEV = ("x", "z")
AXES = ("zh", "y", "c", "x", "z")
EPSILON = 1e-06
RATE = 0.3
MESH = pl.DeviceIdType.MESH
F32, BF16 = jnp.float32, jnp.bfloat16
ROWS, COLS, RANK = 1024, 256, 128
GROUPS = 32
WIDTH = 16 * COLS
GROUP_ROWS, SHARE = 256, 64


def ring_hops(d, n):
    return min(d, n - d)


YC = sorted(
    [(dy, dc) for dy in range(8) for dc in range(2) if dy or dc],
    key=lambda o: -(ring_hops(o[0], 8) + 0.5 * o[1]),
)
ZX = sorted(
    [(dz, dx) for dz in range(8) for dx in range(4) if dz or dx],
    key=lambda o: -(ring_hops(o[0], 8) + ring_hops(o[1], 4)),
)


def split(value):
    high = value.astype(BF16)
    return high, (value - high.astype(F32)).astype(BF16)


def dot3(a, b, dims):
    def dot(left, right):
        return lax.dot_general(left, right, (dims, ((), ())), preferred_element_type=F32)

    return dot(a[0], b[0]) + (dot(a[0], b[1]) + dot(a[1], b[0]))


def shift_down(mixed, count):
    return lax.shift_right_logical(mixed, jnp.full(mixed.shape, count, jnp.int32))


def hashed(mixed):
    mixed = mixed ^ shift_down(mixed, 15)
    mixed = mixed * 73244475
    mixed = mixed ^ shift_down(mixed, 13)
    mixed = mixed * 1911520717
    mixed = mixed ^ shift_down(mixed, 16)
    return (mixed & 65535).astype(F32) * (1.0 / 32768.0) - 1.0


def kernel(
    u_hbm, v_hbm, w_hbm, plan_hbm, seeds_hbm, u_out, v_out,
    u_now, v_now, w_in, plan, seeds,
    scores, u_hi, u_lo, wu_hi, wu_lo, v_hi, v_lo, d_hi, d_lo, wide,
    r_buf, rx, z_src, rz, g_full, v_src, v_got, h_src, h_got,
    n1_src, n1, n2_src, n2,
    in_s, rx_s, rx_r, rz_s, rz_r, az_s, az_r, ax_s, ax_r, sh_s, sh_r, n1_s, n1_r, n2_s, n2_r,
):
    zh, y, c, x, z = (lax.axis_index(a) for a in AXES)
    place = (zh * 8 + y) * 2 + c
    ring_z = zh * 4 + z

    loads = [
        pltpu.make_async_copy(src, dst, in_s.at[i])
        for i, (src, dst) in enumerate(
            [(seeds_hbm, seeds), (plan_hbm, plan), (u_hbm, u_now), (v_hbm, v_now), (w_hbm, w_in)]
        )
    ]
    for load in loads:
        load.start()

    def place_at(by):
        other = lax.rem(place + by + GROUPS, GROUPS)
        return (other // 16, lax.rem(other // 2, 8), lax.rem(other, 2), x, z)

    def yc(offset):
        return (zh, lax.rem(y + offset[0], 8), lax.rem(c + offset[1], 2), x, z)

    def zx(offset):
        other = lax.rem(ring_z + offset[0], 8)
        return (other // 4, y, c, lax.rem(x + offset[1], 4), lax.rem(other, 4))

    def x_at(k):
        return (zh, y, c, lax.rem(x + k, 4), z)

    def z_at(j):
        return (zh, y, c, x, z ^ j)

    def remote(src, dst, s_sem, r_sem, device):
        return pltpu.make_async_remote_copy(
            src_ref=src, dst_ref=dst, send_sem=s_sem, recv_sem=r_sem,
            device_id=device, device_id_type=MESH,
        )

    pending = []

    def send(src, dst, s_sem, r_sem, device):
        copy = remote(src, dst, s_sem, r_sem, device)
        copy.start()
        pending.append(copy)
        return copy

    def settle():
        for copy in pending:
            copy.wait_send()
        pending.clear()

    barrier = pltpu.get_barrier_semaphore()
    for offset in ZX:
        pl.semaphore_signal(barrier, inc=1, device_id=zx(offset), device_id_type=MESH)
    for offset in YC:
        pl.semaphore_signal(barrier, inc=1, device_id=yc(offset), device_id_type=MESH)
    pl.semaphore_signal(barrier, inc=1, device_id=place_at(-1), device_id_type=MESH)
    for load in loads:
        load.wait()

    after = place_at(1)
    own = pl.ds(pl.multiple_of(z * GROUP_ROWS + x * SHARE, SHARE), SHARE)

    def group(j):
        first = pl.multiple_of((z ^ j) * GROUP_ROWS, GROUP_ROWS)
        return first, pl.ds(first, GROUP_ROWS)

    def part(j, k=0):
        return pl.ds(
            pl.multiple_of((z ^ j) * GROUP_ROWS + lax.rem(x + k, 4) * SHARE, SHARE), SHARE
        )

    def score_base(t):
        panel = plan[lax.rem(place - t + GROUPS, GROUPS)]
        seed = seeds[place, panel]
        first_col = panel * WIDTH + (x * 4 + z) * COLS
        base = seed * 374761393 + place * ROWS * 668265263
        return (lax.broadcasted_iota(jnp.int32, (1, COLS), 1) + first_col) * 1274126177 + base

    def score_rows(cols, first, count):
        rows = (lax.broadcasted_iota(jnp.int32, (count, COLS), 0) + first) * 668265263
        return hashed(rows + cols)

    def fill_scores(t):
        cols = score_base(t)
        for block in range(16):
            scores[t - 1, block * 64 : (block + 1) * 64, :] = score_rows(cols, block * 64, 64)

    def keep_u(rows, value):
        u_hi[rows, :], u_lo[rows, :] = split(value)
        wu_hi[rows, :], wu_lo[rows, :] = split(value * wide[rows, :])

    def keep_v(value):
        v_hi[...], v_lo[...] = split(value)

    def v_pair():
        return v_hi[...], v_lo[...]

    def residual(rows, score):
        d = split(score - dot3((u_hi[rows, :], u_lo[rows, :]), v_pair(), ((1,), (1,))))
        d_hi[rows, :], d_lo[rows, :] = d
        return d

    def grad_v():
        return dot3((d_hi[...], d_lo[...]), (wu_hi[...], wu_lo[...]), ((0,), (0,)))

    def send_x(t, j):
        return [
            send(r_buf.at[t, part(j, k)], rx.at[t, j, k - 1], rx_s.at[t, j, k - 1], rx_r.at[t, j, k - 1], x_at(k))
            for k in (2, 1, 3)
        ]

    def collect_x(t, sent_x):
        sent_z = []
        for j in (3, 2, 1, 0):
            for copy in sent_x[j]:
                copy.wait_recv()
            partial = r_buf[t, part(j), :] + (rx[t, j, 0] + rx[t, j, 1] + rx[t, j, 2])
            if j:
                z_src[t, j - 1] = partial
                sent_z.append(
                    send(z_src.at[t, j - 1], rz.at[t, j - 1], rz_s.at[t, j - 1], rz_r.at[t, j - 1], z_at(j))
                )
        return partial, sent_z

    def collect_z(t, partial, sent_z):
        for copy in sent_z:
            copy.wait_recv()
        return partial + (rz[t, 0] + rz[t, 1] + rz[t, 2])

    def gather_z(t):
        return {
            j: send(g_full.at[t, own], g_full.at[t, own], az_s.at[t, j - 1], az_r.at[t, j - 1], z_at(j))
            for j in (3, 2, 1)
        }

    def gather_x(t):
        return [
            send(g_full.at[t, own], g_full.at[t, own], ax_s.at[t, 0, k - 1], ax_r.at[t, 0, k - 1], x_at(k))
            for k in (2, 1, 3)
        ]

    def gather_start(t):
        return gather_z(t), gather_x(t)

    def gather_forward(t, state, j):
        to_z, to_x = state
        to_z[j].wait_recv()
        for k in (2, 1, 3):
            to_x.append(
                send(
                    g_full.at[t, part(j)], g_full.at[t, part(j)],
                    ax_s.at[t, j, k - 1], ax_r.at[t, j, k - 1], x_at(k),
                )
            )

    def gather_end(t, state):
        for copy in state[1]:
            copy.wait_recv()
        return g_full[t]

    def sum_first(i):
        for slot, o in enumerate(YC):
            remote(n1_src.at[i], n1.at[i, slot], n1_s.at[i], n1_r.at[i], yc(o)).start()

    def sum_wait(i, landed, s_sem, r_sem):
        every = remote(landed.at[i], landed.at[i], s_sem.at[i], r_sem.at[i], after)
        every.wait_recv()
        pending.append(every)
        return jnp.sum(landed[i], axis=0)

    def sum_second(i):
        n2_src[i] = n1_src[i] + sum_wait(i, n1, n1_s, n1_r)
        for slot, o in enumerate(ZX):
            remote(n2_src.at[i], n2.at[i, slot], n2_s.at[i], n2_r.at[i], zx(o)).start()

    def sum_end(i):
        return jnp.sum(n2_src[i] + sum_wait(i, n2, n2_s, n2_r), axis=1, keepdims=True)

    def step_u(total):
        return RATE / jnp.sqrt(total[0:1] / float(ROWS * GROUPS * RANK) + EPSILON)

    def step_v(total):
        return RATE / jnp.sqrt(total[1:2] / float(WIDTH * GROUPS * RANK) + EPSILON)

    def squares(value):
        return jnp.sum(value * value, axis=0, keepdims=True)

    for block in range(8):
        row = jnp.broadcast_to(w_in[block : block + 1, :], (128, 128))
        wide[block * 128 : (block + 1) * 128, :] = row.T
    keep_v(v_now[...])

    for t in range(STRATA):
        if t == 0:
            cols = score_base(0)
        else:
            sent_v = send(v_src.at[t] if t else v_now, v_got.at[t], sh_s.at[t, 0], sh_r.at[t, 0], after)
        sent_x = {}
        for j in (3, 2, 1, 0):
            first, rows = group(j)
            if t:
                u_now[rows, :] = u_now[rows, :] + move * g_full[t - 1, rows, :]
            keep_u(rows, u_now[rows, :])
            score = scores[t - 1, rows, :] if t else score_rows(cols, first, GROUP_ROWS)
            d = residual(rows, score)
            r_buf[t, rows, :] = dot3(d, v_pair(), ((1,), (0,)))
            if t == 0 and j == 3:
                pl.semaphore_wait(barrier, len(YC) + len(ZX) + 1)
                sent_v = send(v_now, v_got.at[0], sh_s.at[0, 0], sh_r.at[0, 0], after)
            sent_x[j] = send_x(t, j)
        h = grad_v()
        h_src[t] = h
        n1_src[t, 1:2, :] = squares(h)
        sent_h = send(h_src.at[t], h_got.at[t], sh_s.at[t, 1], sh_r.at[t, 1], after)
        if t + 1 < STRATA:
            fill_scores(t + 1)
        partial, sent_z = collect_x(t, sent_x)
        g = wide[own, :] * collect_z(t, partial, sent_z)
        g_full[t, own, :] = g
        n1_src[t, 0:1, :] = squares(g)
        sum_first(t)
        gather = gather_start(t)
        gather_forward(t, gather, 1)
        gather_forward(t, gather, 2)
        sum_second(t)
        gather_forward(t, gather, 3)
        settle()
        sent_v.wait_recv()
        sent_h.wait_recv()
        g = gather_end(t, gather)
        total = sum_end(t)
        move = step_u(total)
        v = v_got[t] + step_v(total) * h_got[t]
        if t + 1 < STRATA:
            v_src[t + 1] = v
            keep_v(v)
        else:
            v_out[...] = v
            u_out[...] = u_now[...] + move * g
    settle()


def per_device(query_factors, panel_factors, query_weight, plan, tile_seeds):
    vmem = pl.BlockSpec(memory_space=pltpu.VMEM)
    anywhere = pl.BlockSpec(memory_space=pl.ANY)
    dma = pltpu.SemaphoreType.DMA
    T = STRATA
    return pl.pallas_call(
        kernel,
        out_shape=(
            jax.ShapeDtypeStruct((ROWS, RANK), F32),
            jax.ShapeDtypeStruct((COLS, RANK), F32),
        ),
        in_specs=[anywhere] * 5,
        out_specs=(vmem, vmem),
        scratch_shapes=[
            pltpu.VMEM((ROWS, RANK), F32),
            pltpu.VMEM((COLS, RANK), F32),
            pltpu.VMEM((8, RANK), F32),
            pltpu.SMEM((GROUPS,), jnp.int32),
            pltpu.SMEM((GROUPS, GROUPS), jnp.int32),
            pltpu.VMEM((T - 1, ROWS, COLS), F32),
            pltpu.VMEM((ROWS, RANK), BF16),
            pltpu.VMEM((ROWS, RANK), BF16),
            pltpu.VMEM((ROWS, RANK), BF16),
            pltpu.VMEM((ROWS, RANK), BF16),
            pltpu.VMEM((COLS, RANK), BF16),
            pltpu.VMEM((COLS, RANK), BF16),
            pltpu.VMEM((ROWS, COLS), BF16),
            pltpu.VMEM((ROWS, COLS), BF16),
            pltpu.VMEM((ROWS, RANK), F32),
            pltpu.VMEM((T, ROWS, RANK), F32),
            pltpu.VMEM((T, 4, 3, SHARE, RANK), F32),
            pltpu.VMEM((T, 3, SHARE, RANK), F32),
            pltpu.VMEM((T, 3, SHARE, RANK), F32),
            pltpu.VMEM((T, ROWS, RANK), F32),
            pltpu.VMEM((T, COLS, RANK), F32),
            pltpu.VMEM((T, COLS, RANK), F32),
            pltpu.VMEM((T, COLS, RANK), F32),
            pltpu.VMEM((T, COLS, RANK), F32),
            pltpu.VMEM((SUMS, 2, RANK), F32),
            pltpu.VMEM((SUMS, len(YC), 2, RANK), F32),
            pltpu.VMEM((SUMS, 2, RANK), F32),
            pltpu.VMEM((SUMS, len(ZX), 2, RANK), F32),
            dma((5,)),
            dma((T, 4, 3)), dma((T, 4, 3)),
            dma((T, 3)), dma((T, 3)),
            dma((T, 3)), dma((T, 3)),
            dma((T, 4, 3)), dma((T, 4, 3)),
            dma((T, 2)), dma((T, 2)),
            dma((SUMS,)), dma((SUMS,)),
            dma((SUMS,)), dma((SUMS,)),
        ],
        compiler_params=pltpu.CompilerParams(
            collective_id=0, has_side_effects=True, vmem_limit_bytes=56 * 2**20
        ),
        name="strata",
    )(query_factors, panel_factors, query_weight.reshape(8, 128), plan, tile_seeds)


def solution(mesh):
    finer = Mesh(mesh.devices.reshape(2, 8, 2, 4, 4), AXES)
    return jax.shard_map(
        per_device,
        mesh=finer,
        in_specs=(P(PB, None), P(PB + DEV, None), P(PB), P(), P()),
        out_specs=(P(PB, None), P(PB + DEV, None)),
        check_vma=False,
    )
```

```python
import functools

import jax
import jax.numpy as jnp
from jax import lax
from jax.experimental import pallas as pl
from jax.experimental.pallas import tpu as pltpu
from jax.sharding import Mesh
from jax.sharding import PartitionSpec as P

STRATA = 3
SUMS = 3
PB = ("zh", "y", "c")
DEV = ("x", "z")
AXES = ("zh", "y", "c", "x", "z")
EPSILON = 1e-06
RATE = 0.3
MESH = pl.DeviceIdType.MESH
F32, BF16 = jnp.float32, jnp.bfloat16
ROWS, COLS, RANK = 1024, 256, 128
GROUPS = 32
WIDTH = 16 * COLS
GROUP_ROWS, SHARE = 256, 64


def ring_hops(d, n):
    return min(d, n - d)


YC = sorted(
    [(dy, dc) for dy in range(8) for dc in range(2) if dy or dc],
    key=lambda o: -(ring_hops(o[0], 8) + 0.5 * o[1]),
)
ZX = sorted(
    [(dz, dx) for dz in range(8) for dx in range(4) if dz or dx],
    key=lambda o: -(ring_hops(o[0], 8) + ring_hops(o[1], 4)),
)


def split(value):
    high = value.astype(BF16)
    return high, (value - high.astype(F32)).astype(BF16)


def dot3(a, b, dims):
    def dot(left, right):
        return lax.dot_general(left, right, (dims, ((), ())), preferred_element_type=F32)

    return dot(a[0], b[0]) + (dot(a[0], b[1]) + dot(a[1], b[0]))


def shift_down(mixed, count):
    return lax.shift_right_logical(mixed, jnp.full(mixed.shape, count, jnp.int32))


def hashed(mixed):
    mixed = mixed ^ shift_down(mixed, 15)
    mixed = mixed * 73244475
    mixed = mixed ^ shift_down(mixed, 13)
    mixed = mixed * 1911520717
    mixed = mixed ^ shift_down(mixed, 16)
    return (mixed & 65535).astype(F32) * (1.0 / 32768.0) - 1.0


def kernel(
    u_hbm, v_hbm, w_hbm, plan_hbm, seeds_hbm, u_out, v_out,
    u_now, v_now, w_in, plan, seeds,
    scores, u_hi, u_lo, wu_hi, wu_lo, v_hi, v_lo, d_hi, d_lo, wide,
    r_buf, rx, z_src, rz, g_full, v_src, v_got, h_src, h_got,
    n1_src, n1, n2_src, n2,
    in_s, rx_s, rx_r, rz_s, rz_r, az_s, az_r, ax_s, ax_r, sh_s, sh_r, n1_s, n1_r, n2_s, n2_r,
):
    zh, y, c, x, z = (lax.axis_index(a) for a in AXES)
    place = (zh * 8 + y) * 2 + c
    ring_z = zh * 4 + z

    loads = [
        pltpu.make_async_copy(src, dst, in_s.at[i])
        for i, (src, dst) in enumerate(
            [(seeds_hbm, seeds), (plan_hbm, plan), (u_hbm, u_now), (v_hbm, v_now), (w_hbm, w_in)]
        )
    ]
    for load in loads:
        load.start()

    def place_at(by):
        other = lax.rem(place + by + GROUPS, GROUPS)
        return (other // 16, lax.rem(other // 2, 8), lax.rem(other, 2), x, z)

    def yc(offset):
        return (zh, lax.rem(y + offset[0], 8), lax.rem(c + offset[1], 2), x, z)

    def zx(offset):
        other = lax.rem(ring_z + offset[0], 8)
        return (other // 4, y, c, lax.rem(x + offset[1], 4), lax.rem(other, 4))

    def x_at(k):
        return (zh, y, c, lax.rem(x + k, 4), z)

    def z_at(j):
        return (zh, y, c, x, z ^ j)

    def remote(src, dst, s_sem, r_sem, device):
        return pltpu.make_async_remote_copy(
            src_ref=src, dst_ref=dst, send_sem=s_sem, recv_sem=r_sem,
            device_id=device, device_id_type=MESH,
        )

    pending = []

    def send(src, dst, s_sem, r_sem, device):
        copy = remote(src, dst, s_sem, r_sem, device)
        copy.start()
        pending.append(copy)
        return copy

    def settle():
        for copy in pending:
            copy.wait_send()
        pending.clear()

    barrier = pltpu.get_barrier_semaphore()
    for offset in ZX:
        pl.semaphore_signal(barrier, inc=1, device_id=zx(offset), device_id_type=MESH)
    for offset in YC:
        pl.semaphore_signal(barrier, inc=1, device_id=yc(offset), device_id_type=MESH)
    pl.semaphore_signal(barrier, inc=1, device_id=place_at(-1), device_id_type=MESH)
    for load in loads:
        load.wait()

    after = place_at(1)
    own = pl.ds(pl.multiple_of(z * GROUP_ROWS + x * SHARE, SHARE), SHARE)

    def group(j):
        first = pl.multiple_of((z ^ j) * GROUP_ROWS, GROUP_ROWS)
        return first, pl.ds(first, GROUP_ROWS)

    def part(j, k=0):
        return pl.ds(
            pl.multiple_of((z ^ j) * GROUP_ROWS + lax.rem(x + k, 4) * SHARE, SHARE), SHARE
        )

    def score_base(t):
        panel = plan[lax.rem(place - t + GROUPS, GROUPS)]
        seed = seeds[place, panel]
        first_col = panel * WIDTH + (x * 4 + z) * COLS
        base = seed * 374761393 + place * ROWS * 668265263
        return (lax.broadcasted_iota(jnp.int32, (1, COLS), 1) + first_col) * 1274126177 + base

    def score_rows(cols, first, count):
        rows = (lax.broadcasted_iota(jnp.int32, (count, COLS), 0) + first) * 668265263
        return hashed(rows + cols)

    def fill_scores(t):
        cols = score_base(t)
        for block in range(16):
            scores[t - 1, block * 64 : (block + 1) * 64, :] = score_rows(cols, block * 64, 64)

    def keep_u(rows, value):
        u_hi[rows, :], u_lo[rows, :] = split(value)
        wu_hi[rows, :], wu_lo[rows, :] = split(value * wide[rows, :])

    def keep_v(value):
        v_hi[...], v_lo[...] = split(value)

    def v_pair():
        return v_hi[...], v_lo[...]

    def residual(rows, score):
        d = split(score - dot3((u_hi[rows, :], u_lo[rows, :]), v_pair(), ((1,), (1,))))
        d_hi[rows, :], d_lo[rows, :] = d
        return d

    def grad_v():
        return dot3((d_hi[...], d_lo[...]), (wu_hi[...], wu_lo[...]), ((0,), (0,)))

    def send_x(t, j, peers=(2, 1, 3)):
        return [
            send(r_buf.at[t, part(j, k)], rx.at[t, j, k - 1], rx_s.at[t, j, k - 1], rx_r.at[t, j, k - 1], x_at(k))
            for k in peers
        ]

    def collect_x(t, sent_x):
        sent_z = []
        for j in (3, 2, 1, 0):
            for copy in sent_x[j]:
                copy.wait_recv()
            partial = r_buf[t, part(j), :] + (rx[t, j, 0] + rx[t, j, 1] + rx[t, j, 2])
            if j:
                z_src[t, j - 1] = partial
                sent_z.append(
                    send(z_src.at[t, j - 1], rz.at[t, j - 1], rz_s.at[t, j - 1], rz_r.at[t, j - 1], z_at(j))
                )
        return partial, sent_z

    def collect_z(t, partial, sent_z):
        for copy in sent_z:
            copy.wait_recv()
        return partial + (rz[t, 0] + rz[t, 1] + rz[t, 2])

    def gather_z(t):
        return {
            j: send(g_full.at[t, own], g_full.at[t, own], az_s.at[t, j - 1], az_r.at[t, j - 1], z_at(j))
            for j in (3, 2, 1)
        }

    def gather_x(t):
        return [
            send(g_full.at[t, own], g_full.at[t, own], ax_s.at[t, 0, k - 1], ax_r.at[t, 0, k - 1], x_at(k))
            for k in (2, 1, 3)
        ]

    def gather_start(t):
        return gather_z(t), gather_x(t)

    def gather_forward(t, state, j):
        to_z, to_x = state
        to_z[j].wait_recv()
        for k in (2, 1, 3):
            to_x.append(
                send(
                    g_full.at[t, part(j)], g_full.at[t, part(j)],
                    ax_s.at[t, j, k - 1], ax_r.at[t, j, k - 1], x_at(k),
                )
            )

    def gather_end(t, state):
        for copy in state[1]:
            copy.wait_recv()
        return g_full[t]

    def sum_first(i):
        for slot, o in enumerate(YC):
            remote(n1_src.at[i], n1.at[i, slot], n1_s.at[i], n1_r.at[i], yc(o)).start()

    def sum_wait(i, landed, s_sem, r_sem):
        every = remote(landed.at[i], landed.at[i], s_sem.at[i], r_sem.at[i], after)
        every.wait_recv()
        pending.append(every)
        return jnp.sum(landed[i], axis=0)

    def sum_second(i):
        n2_src[i] = n1_src[i] + sum_wait(i, n1, n1_s, n1_r)
        for slot, o in enumerate(ZX):
            remote(n2_src.at[i], n2.at[i, slot], n2_s.at[i], n2_r.at[i], zx(o)).start()

    def sum_end(i):
        return jnp.sum(n2_src[i] + sum_wait(i, n2, n2_s, n2_r), axis=1, keepdims=True)

    def step_u(total):
        return RATE / jnp.sqrt(total[0:1] / float(ROWS * GROUPS * RANK) + EPSILON)

    def step_v(total):
        return RATE / jnp.sqrt(total[1:2] / float(WIDTH * GROUPS * RANK) + EPSILON)

    def squares(value):
        return jnp.sum(value * value, axis=0, keepdims=True)

    for block in range(8):
        row = jnp.broadcast_to(w_in[block : block + 1, :], (128, 128))
        wide[block * 128 : (block + 1) * 128, :] = row.T
    keep_v(v_now[...])

    for t in range(STRATA):
        if t == 0:
            cols = score_base(0)
        else:
            sent_v = send(v_src.at[t] if t else v_now, v_got.at[t], sh_s.at[t, 0], sh_r.at[t, 0], after)
        sent_x = {}
        for j in (3, 2, 1, 0):
            sent_x[j] = []
            for peers in ((2,), (1,), (3,), ()) if j == 3 else ((2, 1, 3),):
                if j == 3:
                    first = pl.multiple_of(
                        (z ^ j) * GROUP_ROWS + lax.rem(x + sum(peers), 4) * SHARE, SHARE
                    )
                    count = SHARE
                else:
                    first, count = group(j)[0], GROUP_ROWS
                rows = pl.ds(first, count)
                if t:
                    u_now[rows, :] = u_now[rows, :] + move * g_full[t - 1, rows, :]
                keep_u(rows, u_now[rows, :])
                score = scores[t - 1, rows, :] if t else score_rows(cols, first, count)
                d = residual(rows, score)
                r_buf[t, rows, :] = dot3(d, v_pair(), ((1,), (0,)))
                if t == 0 and peers == (2,):
                    pl.semaphore_wait(barrier, len(YC) + len(ZX) + 1)
                    sent_v = send(v_now, v_got.at[0], sh_s.at[0, 0], sh_r.at[0, 0], after)
                sent_x[j] += send_x(t, j, peers)
        h = grad_v()
        h_src[t] = h
        n1_src[t, 1:2, :] = squares(h)
        sent_h = send(h_src.at[t], h_got.at[t], sh_s.at[t, 1], sh_r.at[t, 1], after)
        if t + 1 < STRATA:
            fill_scores(t + 1)
        partial, sent_z = collect_x(t, sent_x)
        g = wide[own, :] * collect_z(t, partial, sent_z)
        g_full[t, own, :] = g
        n1_src[t, 0:1, :] = squares(g)
        sum_first(t)
        gather = gather_start(t)
        gather_forward(t, gather, 1)
        gather_forward(t, gather, 2)
        sum_second(t)
        gather_forward(t, gather, 3)
        settle()
        sent_v.wait_recv()
        sent_h.wait_recv()
        g = gather_end(t, gather)
        total = sum_end(t)
        move = step_u(total)
        v = v_got[t] + step_v(total) * h_got[t]
        if t + 1 < STRATA:
            v_src[t + 1] = v
            keep_v(v)
        else:
            v_out[...] = v
            u_out[...] = u_now[...] + move * g
    settle()


def per_device(query_factors, panel_factors, query_weight, plan, tile_seeds):
    vmem = pl.BlockSpec(memory_space=pltpu.VMEM)
    anywhere = pl.BlockSpec(memory_space=pl.ANY)
    dma = pltpu.SemaphoreType.DMA
    T = STRATA
    return pl.pallas_call(
        kernel,
        out_shape=(
            jax.ShapeDtypeStruct((ROWS, RANK), F32),
            jax.ShapeDtypeStruct((COLS, RANK), F32),
        ),
        in_specs=[anywhere] * 5,
        out_specs=(vmem, vmem),
        scratch_shapes=[
            pltpu.VMEM((ROWS, RANK), F32),
            pltpu.VMEM((COLS, RANK), F32),
            pltpu.VMEM((8, RANK), F32),
            pltpu.SMEM((GROUPS,), jnp.int32),
            pltpu.SMEM((GROUPS, GROUPS), jnp.int32),
            pltpu.VMEM((T - 1, ROWS, COLS), F32),
            pltpu.VMEM((ROWS, RANK), BF16),
            pltpu.VMEM((ROWS, RANK), BF16),
            pltpu.VMEM((ROWS, RANK), BF16),
            pltpu.VMEM((ROWS, RANK), BF16),
            pltpu.VMEM((COLS, RANK), BF16),
            pltpu.VMEM((COLS, RANK), BF16),
            pltpu.VMEM((ROWS, COLS), BF16),
            pltpu.VMEM((ROWS, COLS), BF16),
            pltpu.VMEM((ROWS, RANK), F32),
            pltpu.VMEM((T, ROWS, RANK), F32),
            pltpu.VMEM((T, 4, 3, SHARE, RANK), F32),
            pltpu.VMEM((T, 3, SHARE, RANK), F32),
            pltpu.VMEM((T, 3, SHARE, RANK), F32),
            pltpu.VMEM((T, ROWS, RANK), F32),
            pltpu.VMEM((T, COLS, RANK), F32),
            pltpu.VMEM((T, COLS, RANK), F32),
            pltpu.VMEM((T, COLS, RANK), F32),
            pltpu.VMEM((T, COLS, RANK), F32),
            pltpu.VMEM((SUMS, 2, RANK), F32),
            pltpu.VMEM((SUMS, len(YC), 2, RANK), F32),
            pltpu.VMEM((SUMS, 2, RANK), F32),
            pltpu.VMEM((SUMS, len(ZX), 2, RANK), F32),
            dma((5,)),
            dma((T, 4, 3)), dma((T, 4, 3)),
            dma((T, 3)), dma((T, 3)),
            dma((T, 3)), dma((T, 3)),
            dma((T, 4, 3)), dma((T, 4, 3)),
            dma((T, 2)), dma((T, 2)),
            dma((SUMS,)), dma((SUMS,)),
            dma((SUMS,)), dma((SUMS,)),
        ],
        compiler_params=pltpu.CompilerParams(
            collective_id=0, has_side_effects=True, vmem_limit_bytes=56 * 2**20
        ),
        name="strata",
    )(query_factors, panel_factors, query_weight.reshape(8, 128), plan, tile_seeds)


def solution(mesh):
    finer = Mesh(mesh.devices.reshape(2, 8, 2, 4, 4), AXES)
    return jax.shard_map(
        per_device,
        mesh=finer,
        in_specs=(P(PB, None), P(PB + DEV, None), P(PB), P(), P()),
        out_specs=(P(PB, None), P(PB + DEV, None)),
        check_vma=False,
    )
```
